32 devices in a mesh: outer: 4 (over y, x), inner: 8 (over z, core).
Axes of the slice: x: 2, y: 2, z: 4, core: 2. Of those that a mesh axis runs over, the one named last changes fastest.
Arguments:
- tokens: bfloat16 [512, 8192], P(None, 'outer'), may hold values from -60 to 60
- base_gate: bfloat16 [8192, 28672], P('outer', 'inner'), may hold values from -0.06629126 to 0.06629126
- base_up: bfloat16 [8192, 28672], P('outer', 'inner'), may hold values from -0.06629126 to 0.06629126
- adjusted_gate: bfloat16 [8192, 28672], P('outer', 'inner'), may hold values from -0.092807765 to 0.092807765
- adjusted_up: bfloat16 [8192, 28672], P('outer', 'inner'), may hold values from -0.092807765 to 0.092807765
- slab_block: int32 [8], replicated, may hold values from 0 to 7, each once
Outputs:
- correlation: float32 [3584, 28672], P('outer', 'inner')
The draws below stay inside these ranges and needn't reach their ends.
Inputs may be any that keep to these rules, and one draw needn't show every extreme that they name: `slab_block`: each block number appears once.
All inputs are finite; a program needn't handle non-finite values.
Results may differ from the reference program's by a relative error of at most 0.004.
Values may be sent and summed in bfloat16 or wider, within the bound.
A program may use at most 192 MiB of HBM per device.

```python
import jax
import jax.numpy as jnp
from jax import lax

D = 8192
FF = 28672
TOKENS = 512
SLAB = 3584
N_INNER = 8


def weight_pair(key, tag):
    inner_key = jax.random.fold_in(key, tag)
    base = jnp.clip(jax.random.normal(jax.random.fold_in(inner_key, 0), (D, FF), jnp.float32), -6.0, 6.0)
    fresh = jnp.clip(jax.random.normal(jax.random.fold_in(inner_key, 1), (D, FF), jnp.float32), -6.0, 6.0)
    scale = D ** (-0.5)
    return (base * scale, (0.8 * base + 0.6 * fresh) * scale)


def draw_base_gate(key, part):
    return weight_pair(key, 11)[0].astype(jnp.bfloat16)


def draw_adjusted_gate(key, part):
    return weight_pair(key, 11)[1].astype(jnp.bfloat16)


def draw_base_up(key, part):
    return weight_pair(key, 23)[0].astype(jnp.bfloat16)


def draw_adjusted_up(key, part):
    return weight_pair(key, 23)[1].astype(jnp.bfloat16)


def draw_tokens(key, part):
    inner_key = jax.random.fold_in(key, 37)
    ramp = jnp.arange(TOKENS, dtype=jnp.float32)[:, None] / max(TOKENS - 1, 1)
    spread = jax.random.uniform(jax.random.fold_in(inner_key, 0), (TOKENS, 1), jnp.float32)
    row_scale = jnp.exp(jnp.log(3.0) * ramp + jnp.log(10.0 / 3.0) * spread)
    values = jnp.clip(jax.random.normal(jax.random.fold_in(inner_key, 1), (TOKENS, D), jnp.float32), -6.0, 6.0)
    return (values * row_scale).astype(jnp.bfloat16)


def setup_inputs(seed: int = 0) -> dict:
    key_of = jax.random.split(jax.random.key(seed), 7)
    return {
        "tokens": draw_tokens(jax.random.fold_in(key_of[6], 71), 0),
        "base_gate": draw_base_gate(jax.random.fold_in(key_of[6], 71), 0),
        "base_up": draw_base_up(jax.random.fold_in(key_of[6], 71), 0),
        "adjusted_gate": draw_adjusted_gate(jax.random.fold_in(key_of[6], 71), 0),
        "adjusted_up": draw_adjusted_up(jax.random.fold_in(key_of[6], 71), 0),
        "slab_block": jax.random.permutation(key_of[5], N_INNER).astype(jnp.int32),
    }


def scores(tokens, gate_weight, up_weight):
    gate = jnp.dot(tokens, gate_weight, preferred_element_type=jnp.float32)
    up = jnp.dot(tokens, up_weight, preferred_element_type=jnp.float32)
    hidden = jax.nn.silu(gate) * up
    mean = lax.optimization_barrier(jnp.mean(hidden, axis=0, keepdims=True))
    var = lax.optimization_barrier(jnp.mean((hidden - mean) ** 2, axis=0, keepdims=True))
    return ((hidden - mean) * lax.rsqrt(var + 1e-05)).astype(jnp.bfloat16)

def reference(tokens, base_gate, base_up, adjusted_gate, adjusted_up, slab_block):
    base_scores = scores(tokens, base_gate, base_up)
    adjusted_scores = scores(tokens, adjusted_gate, adjusted_up)
    start = (slab_block[0] * SLAB).astype(jnp.int32)
    slab = lax.dynamic_slice_in_dim(base_scores, start, SLAB, 1)
    gram = lax.dot_general(slab, adjusted_scores, (((0,), (0,)), ((), ())), preferred_element_type=jnp.float32)
    return gram / TOKENS
```

```python
import jax
import jax.numpy as jnp
from jax import lax
from jax.sharding import PartitionSpec as P

WIRE = jnp.float16


def swap(value, axis, bit):
    size = lax.axis_size(axis)
    return lax.ppermute(value, axis, [(i, i ^ bit) for i in range(size)])


def bits_of(size):
    bits = []
    while (1 << len(bits)) < size:
        bits.append(1 << len(bits))
    return bits


def halve(block, axis, bits):
    size = lax.axis_size(axis)
    me = lax.axis_index(axis)
    held = {m: block(me ^ m) for m in range(size)}
    live = list(range(size))
    for bit in bits:
        keep = [m for m in live if not m & bit]
        got = {m: swap(held[m ^ bit].astype(WIRE), axis, bit) for m in reversed(keep)}
        held = {m: held[m].astype(jnp.float32) + got[m].astype(jnp.float32) for m in keep}
        live = keep
    return held[0]


def double(value, axis, bits):
    held = {0: value}
    for bit in bits:
        held.update({m ^ bit: swap(v, axis, bit) for m, v in list(held.items())})
    return held


def scores(gate, up):
    hidden = jax.nn.silu(gate) * up
    mean = jnp.mean(hidden, axis=0, keepdims=True)
    centered = hidden - mean
    var = jnp.mean(centered * centered, axis=0, keepdims=True)
    return (centered * lax.rsqrt(var + 1e-05)).astype(jnp.bfloat16)


def local(tokens, base_gate, base_up, adjusted_gate, adjusted_up, slab_block):
    units = base_gate.shape[1]
    total_tokens = tokens.shape[0]
    outer_count = lax.axis_size("outer")
    inner_count = lax.axis_size("inner")
    outer = lax.axis_index("outer")
    inner = lax.axis_index("inner")
    width = units // outer_count
    bits = bits_of(outer_count)
    back = bits[::-1]

    def term(weight):
        def block(b):
            part = lax.dynamic_slice_in_dim(weight, b * width, width, 1)
            return jnp.dot(tokens, part, preferred_element_type=jnp.float32).astype(WIRE)
        return block

    def multiply(gate, up):
        return tuple(
            jnp.dot(tokens, w, preferred_element_type=jnp.float32).astype(WIRE)
            for w in (gate, up)
        )

    def nothing(gate, up):
        return tuple(jnp.zeros((total_tokens, units), WIRE) for _ in range(2))

    slab_gate, slab_up = lax.cond(
        inner == slab_block[0], multiply, nothing, base_gate, base_up
    )
    core = inner % 2
    mine = jnp.where(core == 0, slab_gate, slab_up)
    other = jnp.where(core == 0, slab_up, slab_gate)
    mine = mine + swap(other, "inner", 1)

    def slab_term(b):
        return lax.dynamic_slice_in_dim(mine, b * width, width, 1)

    half = total_tokens // 2
    slab_sum = jnp.concatenate(
        [
            halve(lambda b: slab_term(b)[:half], "outer", bits),
            halve(lambda b: slab_term(b)[half:], "outer", back),
        ],
        axis=0,
    )
    across = swap(slab_sum, "inner", 1)
    slab = scores(
        jnp.where(core == 0, slab_sum, across), jnp.where(core == 0, across, slab_sum)
    )
    here = (inner // 2) == (slab_block[0] // 2)
    part = lax.dynamic_slice_in_dim(slab, core * half, half, 0)
    part = jnp.where(here, part, jnp.zeros_like(part))
    for bit in bits_of(inner_count)[1:]:
        part = part + swap(part, "inner", bit)
    rest = swap(part, "inner", 1)
    slab_full = jnp.where(
        core == 0,
        jnp.concatenate([part, rest], axis=0),
        jnp.concatenate([rest, part], axis=0),
    )

    gate = halve(term(adjusted_gate), "outer", bits)
    up = halve(term(adjusted_up), "outer", back)
    adjusted = scores(gate, up)
    top = double(adjusted[:half], "outer", bits)
    bottom = double(adjusted[half:], "outer", back)
    full = jnp.zeros((total_tokens, units), jnp.bfloat16)
    for m in range(outer_count):
        for start, blocks in ((0, top), (half, bottom)):
            full = lax.dynamic_update_slice(full, blocks[m], (start, (outer ^ m) * width))
    gram = lax.dot_general(
        slab_full, full, (((0,), (0,)), ((), ())), preferred_element_type=jnp.float32
    )
    return gram / total_tokens


def solution(mesh):
    return jax.shard_map(
        local,
        mesh=mesh,
        in_specs=(
            P(None, "outer"),
            P("outer", "inner"),
            P("outer", "inner"),
            P("outer", "inner"),
            P("outer", "inner"),
            P(),
        ),
        out_specs=P("outer", "inner"),
        check_vma=False,
    )
```

```python
import jax
import jax.numpy as jnp
from jax import lax
from jax.sharding import PartitionSpec as P

WIRE = jnp.float16


def bits_of(size):
    bits = []
    while (1 << len(bits)) < size:
        bits.append(1 << len(bits))
    return bits


def swap(value, axis, bit):
    size = lax.axis_size(axis)
    return lax.ppermute(value, axis, [(i, i ^ bit) for i in range(size)])


class Path:
    def __init__(self, even, odd):
        self.orders = (even, odd)
        self.size = lax.axis_size("outer")
        self.me = lax.axis_index("outer")
        core = lax.axis_index("inner") % 2
        self.bits = [
            a if a == b else jnp.where(core == 0, a, b) for a, b in zip(even, odd)
        ]

    def index(self, label):
        found = self.me
        for step, bit in enumerate(self.bits):
            if label >> step & 1:
                found = found ^ bit
        return found

    def swap(self, value, step):
        inner_count = lax.axis_size("inner")
        pairs = [
            (o * inner_count + i, (o ^ self.orders[i % 2][step]) * inner_count + i)
            for o in range(self.size)
            for i in range(inner_count)
        ]
        return lax.ppermute(value, ("outer", "inner"), pairs)

    def receive(self, held, step):
        bit = 1 << step
        keep = [label for label in range(self.size) if not label % (2 * bit)]
        return {k: self.swap(held[k ^ bit].astype(WIRE), step) for k in reversed(keep)}

    def add(self, held, got):
        return {k: held[k].astype(jnp.float32) + got[k].astype(jnp.float32) for k in got}

    def halve(self, held, start=0):
        for step in range(start, len(self.bits)):
            held = self.add(held, self.receive(held, step))
        return held[0]

    def double(self, value):
        held = {0: value}
        for step in range(len(self.bits)):
            bit = 1 << step
            held.update({k ^ bit: self.swap(v, step) for k, v in list(held.items())})
        return held


def scores(gate, up):
    hidden = jax.nn.silu(gate) * up
    mean = jnp.mean(hidden, axis=0, keepdims=True)
    centered = hidden - mean
    var = jnp.mean(centered * centered, axis=0, keepdims=True)
    return (centered * lax.rsqrt(var + 1e-05)).astype(jnp.bfloat16)


def local(tokens, base_gate, base_up, adjusted_gate, adjusted_up, slab_block):
    units = base_gate.shape[1]
    total_tokens = tokens.shape[0]
    outer_count = lax.axis_size("outer")
    inner = lax.axis_index("inner")
    core = inner % 2
    width = units // outer_count
    half = total_tokens // 2
    bits = bits_of(outer_count)
    back = bits[::-1]
    gate_path, up_path, core_path = Path(bits, bits), Path(back, back), Path(bits, back)

    def columns(array, block):
        return lax.dynamic_slice_in_dim(array, block * width, width, 1)

    def term(tokens, weight, block):
        return jnp.dot(
            tokens, columns(weight, block), preferred_element_type=jnp.float32
        ).astype(WIRE)

    fence = lax.optimization_barrier

    gate_terms, up_terms = {}, {}
    order = [k for k in reversed(range(outer_count)) if k & 1]
    order += [k for k in reversed(range(2, outer_count)) if not k & 1]
    for label in order:
        gate_terms[label] = fence(term(tokens, adjusted_gate, gate_path.index(label)))
        up_terms[label] = fence(term(tokens, adjusted_up, up_path.index(label)))
    gate_got = gate_path.receive(gate_terms, 0)
    up_got = up_path.receive(up_terms, 0)
    gate_own, up_own = gate_got.pop(0), up_got.pop(0)
    first, gate_got, up_got, _ = fence(
        (tokens, gate_got, up_got, (gate_terms, up_terms))
    )

    holds = inner == slab_block[0]

    def product(tokens, weight):
        full = jnp.dot(tokens, weight, preferred_element_type=jnp.float32)
        return jnp.where(holds, full, 0.0).astype(WIRE)

    evens = range(0, lax.axis_size("inner"), 2)
    slab_gate = product(first, base_gate)
    second, gate_own, up_own, slab_gate = fence((first, gate_own, up_own, slab_gate))
    given_gate = lax.ppermute(slab_gate, "inner", [(i + 1, i) for i in evens])
    slab_up = product(second, base_up)
    gate_held = gate_path.add(gate_terms, gate_got)
    up_held = up_path.add(up_terms, up_got)
    gate_got = gate_path.receive(gate_held, 1)
    up_got = up_path.receive(up_held, 1)
    last, slab_up, given_gate, gate_got, up_got = fence(
        (second, slab_up, given_gate, gate_got, up_got)
    )
    given_up = lax.ppermute(slab_up, "inner", [(i, i + 1) for i in evens])
    gate_terms[0] = term(last, adjusted_gate, gate_path.index(0))
    up_terms[0] = term(last, adjusted_up, up_path.index(0))
    given_up, gate_terms[0] = fence((given_up, gate_terms[0]))
    gate_held[0] = gate_terms[0].astype(jnp.float32) + gate_own.astype(jnp.float32)
    up_held[0] = up_terms[0].astype(jnp.float32) + up_own.astype(jnp.float32)

    def slab_term(label):
        block = core_path.index(label)
        return jnp.where(
            core == 0,
            columns(slab_gate, block) + columns(given_gate, block),
            columns(slab_up, block) + columns(given_up, block),
        )

    slab_sum = core_path.halve({label: slab_term(label) for label in range(outer_count)})

    gate = gate_path.halve(gate_path.add(gate_held, gate_got), 2)
    up = up_path.halve(up_path.add(up_held, up_got), 2)
    adjusted = scores(gate, up)
    blocks = core_path.double(adjusted)

    across = swap(slab_sum, "inner", 1)
    slab = scores(
        jnp.where(core == 0, slab_sum, across), jnp.where(core == 0, across, slab_sum)
    )
    here = (inner // 2) == (slab_block[0] // 2)
    part = lax.dynamic_slice_in_dim(slab, core * half, half, 0)
    part = jnp.where(here, part, jnp.zeros_like(part))
    for bit in bits_of(lax.axis_size("inner"))[1:]:
        part = part + swap(part, "inner", bit)
    rest = swap(part, "inner", 1)
    slab_full = jnp.where(
        core == 0,
        jnp.concatenate([part, rest], axis=0),
        jnp.concatenate([rest, part], axis=0),
    )

    full = jnp.zeros((total_tokens, units), jnp.bfloat16)
    for label in range(outer_count):
        full = lax.dynamic_update_slice(
            full, blocks[label], (0, core_path.index(label) * width)
        )
    gram = lax.dot_general(
        slab_full, full, (((0,), (0,)), ((), ())), preferred_element_type=jnp.float32
    )
    return gram / total_tokens


def solution(mesh):
    return jax.shard_map(
        local,
        mesh=mesh,
        in_specs=(
            P(None, "outer"),
            P("outer", "inner"),
            P("outer", "inner"),
            P("outer", "inner"),
            P("outer", "inner"),
            P(),
        ),
        out_specs=P("outer", "inner"),
        check_vma=False,
    )
```

```python
import jax
import jax.numpy as jnp
from jax import lax
from jax.sharding import PartitionSpec as P

WIRE = jnp.float16


def bits_of(size):
    bits = []
    while (1 << len(bits)) < size:
        bits.append(1 << len(bits))
    return bits


def swap(value, axis, bit):
    size = lax.axis_size(axis)
    return lax.ppermute(value, axis, [(i, i ^ bit) for i in range(size)])


class Path:
    def __init__(self, even, odd):
        self.orders = (even, odd)
        self.size = lax.axis_size("outer")
        self.me = lax.axis_index("outer")
        core = lax.axis_index("inner") % 2
        self.bits = [
            a if a == b else jnp.where(core == 0, a, b) for a, b in zip(even, odd)
        ]

    def index(self, label):
        found = self.me
        for step, bit in enumerate(self.bits):
            if label >> step & 1:
                found = found ^ bit
        return found

    def swap(self, value, step):
        inner_count = lax.axis_size("inner")
        pairs = [
            (o * inner_count + i, (o ^ self.orders[i % 2][step]) * inner_count + i)
            for o in range(self.size)
            for i in range(inner_count)
        ]
        return lax.ppermute(value, ("outer", "inner"), pairs)

    def receive(self, held, step):
        bit = 1 << step
        keep = [label for label in range(self.size) if not label % (2 * bit)]
        return {k: self.swap(held[k ^ bit].astype(WIRE), step) for k in reversed(keep)}

    def add(self, held, got):
        return {k: held[k].astype(jnp.float32) + got[k].astype(jnp.float32) for k in got}

    def halve(self, held, start=0):
        for step in range(start, len(self.bits)):
            held = self.add(held, self.receive(held, step))
        return held[0]

    def double(self, held, start):
        for step in range(start, len(self.bits)):
            bit = 1 << step
            held.update({k ^ bit: self.swap(v, step) for k, v in list(held.items())})
        return held


def scores(gate, up):
    hidden = jax.nn.silu(gate) * up
    mean = jnp.mean(hidden, axis=0, keepdims=True)
    centered = hidden - mean
    var = jnp.mean(centered * centered, axis=0, keepdims=True)
    return (centered * lax.rsqrt(var + 1e-05)).astype(jnp.bfloat16)


def local(tokens, base_gate, base_up, adjusted_gate, adjusted_up, slab_block):
    units = base_gate.shape[1]
    total_tokens = tokens.shape[0]
    outer_count = lax.axis_size("outer")
    inner = lax.axis_index("inner")
    core = inner % 2
    width = units // outer_count
    half = total_tokens // 2
    bits = bits_of(outer_count)
    back = bits[::-1]
    gate_path, up_path, core_path = Path(bits, bits), Path(back, back), Path(bits, back)

    def columns(array, block):
        return lax.dynamic_slice_in_dim(array, block * width, width, 1)

    def term(tokens, weight, block):
        return jnp.dot(
            tokens, columns(weight, block), preferred_element_type=jnp.float32
        ).astype(WIRE)

    fence = lax.optimization_barrier

    holds = inner == slab_block[0]

    def product(tokens, weight):
        full = jnp.dot(tokens, weight, preferred_element_type=jnp.float32)
        return jnp.where(holds, full, 0.0).astype(WIRE)

    gate_terms, up_terms = {}, {}
    leave = [label for label in reversed(range(outer_count)) if label & 1]
    now = tokens
    for label in leave:
        if label == 1:
            slab_gate = product(now, base_gate)
            now, slab_gate = fence((now, slab_gate))
        gate_terms[label] = fence(term(now, adjusted_gate, gate_path.index(label)))
        up_terms[label] = fence(term(now, adjusted_up, up_path.index(label)))
        now, _ = fence((now, (gate_terms, up_terms)))
    gate_got = gate_path.receive(gate_terms, 0)
    up_got = up_path.receive(up_terms, 0)
    gate_own, up_own = gate_got.pop(0), up_got.pop(0)

    for label in reversed(range(2, outer_count, 2)):
        gate_terms[label] = fence(term(now, adjusted_gate, gate_path.index(label)))
        up_terms[label] = fence(term(now, adjusted_up, up_path.index(label)))
    now, gate_got, up_got, _ = fence((now, gate_got, up_got, (gate_terms, up_terms)))
    slab_up = product(now, base_up)
    third, slab_gate, slab_up, gate_own, up_own = fence(
        (now, slab_gate, slab_up, gate_own, up_own)
    )
    given_gate = swap(slab_gate, "inner", 1)
    given_up = swap(slab_up, "inner", 1)
    gate_held = gate_path.add(gate_terms, gate_got)
    up_held = up_path.add(up_terms, up_got)
    gate_sent = {k: fence(v.astype(WIRE)) for k, v in gate_held.items() if k & 2}
    up_sent = {k: fence(v.astype(WIRE)) for k, v in up_held.items() if k & 2}
    gate_got = gate_path.receive(gate_sent, 1)
    up_got = up_path.receive(up_sent, 1)
    last, _ = fence((third, (gate_sent, up_sent)))
    gate_terms[0] = term(last, adjusted_gate, gate_path.index(0))
    up_terms[0] = term(last, adjusted_up, up_path.index(0))
    given_gate, given_up, gate_got, up_got, gate_terms, up_terms = fence(
        (given_gate, given_up, gate_got, up_got, gate_terms, up_terms)
    )
    gate_held[0] = gate_terms[0].astype(jnp.float32) + gate_own.astype(jnp.float32)
    up_held[0] = up_terms[0].astype(jnp.float32) + up_own.astype(jnp.float32)

    def slab_term(label):
        block = core_path.index(label)
        return jnp.where(
            core == 0,
            columns(slab_gate, block) + columns(given_gate, block),
            columns(slab_up, block) + columns(given_up, block),
        )

    slab_held = {label: slab_term(label) for label in range(outer_count)}
    slab_held = core_path.add(slab_held, core_path.receive(slab_held, 0))
    slab_sent = {k: fence(v.astype(WIRE)) for k, v in slab_held.items() if k & 2}
    slab_got = core_path.receive(slab_sent, 1)

    gate = gate_path.halve(gate_path.add(gate_held, gate_got), 2)
    up = up_path.halve(up_path.add(up_held, up_got), 2)
    adjusted, _ = fence((scores(gate, up), slab_sent))
    blocks = {0: adjusted, 1: core_path.swap(adjusted, 0)}
    slab_got = fence((slab_got, adjusted))[0]
    slab_sum = core_path.halve(core_path.add(slab_held, slab_got), 2)

    across = swap(slab_sum, "inner", 1)
    slab = scores(
        jnp.where(core == 0, slab_sum, across), jnp.where(core == 0, across, slab_sum)
    )
    here = (inner // 2) == (slab_block[0] // 2)
    part = lax.dynamic_slice_in_dim(slab, core * half, half, 0)
    part = jnp.where(here, part, jnp.zeros_like(part))
    for bit in bits_of(lax.axis_size("inner"))[1:]:
        part = part + swap(part, "inner", bit)
        if bit == 2:
            blocks[1] = fence((blocks[1], part))[0]
    blocks = core_path.double(blocks, 1)
    rest = swap(part, "inner", 1)
    slab_full = jnp.where(
        core == 0,
        jnp.concatenate([part, rest], axis=0),
        jnp.concatenate([rest, part], axis=0),
    )

    full = jnp.zeros((total_tokens, units), jnp.bfloat16)
    for label in range(outer_count):
        full = lax.dynamic_update_slice(
            full, blocks[label], (0, core_path.index(label) * width)
        )
    gram = lax.dot_general(
        slab_full, full, (((0,), (0,)), ((), ())), preferred_element_type=jnp.float32
    )
    return gram / total_tokens


def solution(mesh):
    return jax.shard_map(
        local,
        mesh=mesh,
        in_specs=(
            P(None, "outer"),
            P("outer", "inner"),
            P("outer", "inner"),
            P("outer", "inner"),
            P("outer", "inner"),
            P(),
        ),
        out_specs=P("outer", "inner"),
        check_vma=False,
    )
```
